32 devices in a mesh: dp: 16 (over z, y, x), mp: 2 (over core).
Axes of the slice: x: 2, y: 2, z: 4, core: 2. Of those that a mesh axis runs over, the one named last changes fastest.
Arguments:
- activations: bfloat16 [8192, 8192], P('dp', 'mp'), may hold values from -6 to 6
- out_grads: bfloat16 [8192, 8192], P('dp', 'mp'), may hold values from -0.09375 to 0.09375
- basis: bfloat16 [8192, 1024], P('mp'), may hold values from -0.0625 to 0.0625
- moment1: float32 [8192, 1024], P(('mp', 'dp')), may hold values from -1.5 to 1.5
- moment2: float32 [8192, 1024], P(('mp', 'dp')), may hold values from 0.0005 to 0.005
Outputs:
- new_first: float32 [8192, 1024], P(('mp', 'dp'))
- new_second: float32 [8192, 1024], P(('mp', 'dp'))
- update: bfloat16 [2, 4096, 8192], P(None, 'dp', 'mp')
The draws below stay inside these ranges and needn't reach their ends.
All inputs are finite; a program needn't handle non-finite values.
Results may differ from the reference program's by a relative error of at most 0.0055.
Values may be sent and summed in bfloat16 or wider, within the bound.
No kernel may reach another device: no remote copies, remote signals or barrier semaphores. Data moves between devices by JAX's collectives and lax.ppermute only.
A program may use at most 128 MiB of HBM per device.

```python
import math
import jax
import jax.numpy as jnp
from jax import lax

D = 8192
NOUT = 8192
R = 1024
STEP = 100
TOKENS = 8192
N_MP = 2


def raised(array, rng, source, target, blocks, factor):
    owner, partner = [(jnp.arange(array.shape[axis_at]) // (array.shape[axis_at] // blocks)).reshape([-1 if axis == axis_at else 1 for axis in range(array.ndim)]) for axis_at in (source, target)]
    chosen = jax.random.permutation(rng, blocks)[partner]
    strong = (owner == chosen) | (owner == (partner + blocks // 2) % blocks)
    return jnp.where(strong, factor * array, array)


def shard_levels(stream_key, shape, pieces, low, high):
    loudness, own = 1.0, jax.random.fold_in(stream_key, 6)
    for position, shards_of in pieces:
        draws = jnp.exp(jax.random.uniform(jax.random.fold_in(own, position), (shards_of,), jnp.float32, low / len(pieces), high / len(pieces)))
        loudness = loudness * jnp.repeat(draws, shape[position] // shards_of).reshape([-1 if axis == position else 1 for axis in range(len(shape))])
    return loudness


def scatter_about(rng, extent, deviation, limit, pieces=(), kind=jnp.bfloat16):
    level = shard_levels(rng, extent, pieces, -0.22, 0.18) if pieces else 1.0
    array = jax.random.normal(rng, extent, jnp.float32) * deviation * level
    return jnp.minimum(jnp.maximum(array, -limit), limit).astype(kind)


def gaussian_with(own_key, shape, width, limit, split, heavy, kind=jnp.bfloat16):
    result = width * jax.random.normal(own_key, shape, jnp.float32)
    if split:
        result = result * shard_levels(own_key, shape, split, -0.22, 0.18)
    return jnp.clip(raised(result, jax.random.fold_in(own_key, 3), *heavy), -limit, limit).astype(kind)


def setup_inputs(seed: int = 0) -> dict:
    key_of = jax.random.split(jax.random.key(seed), 6)
    activations = scatter_about(key_of[0], (TOKENS, D), 1.0, 6.0, ((0, 16), (1, 2)))
    out_grads = gaussian_with(key_of[1], (TOKENS, NOUT), TOKENS ** -0.5, 0.09375, ((0, 16), (1, 2)), (0, 1, 16, 2.0))
    basis = scatter_about(key_of[2], (D, R), D ** -0.5, 0.0625, ((0, 2),))
    moment1 = scatter_about(key_of[3], (NOUT, R), 0.1, 1.5, ((0, 32),), jnp.float32)
    moment2 = jnp.clip(jnp.exp(math.log(0.005) - 2.30258502 * jax.random.uniform(key_of[4], (NOUT, R), jnp.float32) ** shard_levels(key_of[4], (NOUT, R), ((0, 32),), -0.2, 0.2)), 0.0005, 0.005)
    return {"activations": activations, "out_grads": out_grads, "basis": basis, "moment1": moment1, "moment2": moment2}


beta_first = 0.9
beta_second = 0.999
epsilon = 1e-08

def reference(activations, out_grads, basis, moment1, moment2):
    highest = lax.Precision.HIGHEST
    basis_wide = basis.astype(jnp.float32)
    token_rank = jnp.dot(activations.astype(jnp.float32), basis_wide, precision=highest, preferred_element_type=jnp.float32).astype(jnp.bfloat16)
    reduced = jnp.dot(out_grads.astype(jnp.float32).T, token_rank.astype(jnp.float32), precision=highest, preferred_element_type=jnp.float32)
    new_first = beta_first * moment1 + (1.0 - beta_first) * reduced
    new_second = beta_second * moment2 + (1.0 - beta_second) * reduced * reduced
    bias_first = 1.0 - beta_first ** STEP
    bias_second = 1.0 - beta_second ** STEP
    normed = (new_first / bias_first / (jnp.sqrt(new_second / bias_second) + epsilon)).astype(jnp.bfloat16)
    full = jnp.dot(normed.astype(jnp.float32), basis_wide.T, precision=highest, preferred_element_type=jnp.float32).astype(jnp.bfloat16)
    update = full.reshape(N_MP, NOUT // N_MP, D)
    return (new_first, new_second, update)
```

```python
import jax
import jax.numpy as jnp
import numpy as np
from jax import lax
from jax.experimental import pallas as pl
from jax.experimental.pallas import tpu as pltpu
from jax.sharding import PartitionSpec as P

STEP = 100


beta_first = 0.9
beta_second = 0.999
epsilon = 1e-08

VMEM_LIMIT = 48 * 1024 * 1024


def adam(reduced, moment1, moment2):
    new_first = beta_first * moment1 + (1.0 - beta_first) * reduced
    new_second = beta_second * moment2 + (1.0 - beta_second) * reduced * reduced
    bias_first = 1.0 - beta_first**STEP
    bias_second = 1.0 - beta_second**STEP
    normed = (new_first / bias_first / (jnp.sqrt(new_second / bias_second) + epsilon)).astype(
        jnp.bfloat16
    )
    return new_first, new_second, normed


def plain(activations, out_grads, basis, moment1, moment2):
    partial_rank = jnp.dot(activations, basis, preferred_element_type=jnp.float32)
    token_rank = lax.psum(partial_rank, "mp").astype(jnp.bfloat16)
    reduced = lax.psum_scatter(
        lax.dot_general(
            out_grads, token_rank, (((0,), (0,)), ((), ())), preferred_element_type=jnp.float32
        ),
        "dp",
        scatter_dimension=0,
        tiled=True,
    )
    new_first, new_second, normed = adam(reduced, moment1, moment2)
    gathered = lax.all_gather(normed[None], "mp", axis=0, tiled=True)
    groups, owned, ranks = gathered.shape
    full = lax.dot_general(
        gathered.reshape(groups * owned, ranks),
        basis,
        (((1,), (1,)), ((), ())),
        preferred_element_type=jnp.float32,
    )
    return new_first, new_second, full.astype(jnp.bfloat16).reshape(groups, owned, basis.shape[0])


def params(**more):
    return pltpu.CompilerParams(vmem_limit_bytes=VMEM_LIMIT, **more)


def rank_half(half, activations, basis, steps=4):
    tokens, depth = activations.shape
    ranks = basis.shape[1]
    rows, tile = tokens // 2, depth // steps

    def kernel(half_ref, a_ref, b_ref, o_ref):
        part = jnp.dot(a_ref[...], b_ref[...], preferred_element_type=jnp.float32)

        @pl.when(pl.program_id(0) == 0)
        def _():
            o_ref[...] = part

        @pl.when(pl.program_id(0) > 0)
        def _():
            o_ref[...] += part

    return pl.pallas_call(
        kernel,
        out_shape=jax.ShapeDtypeStruct((rows, ranks), jnp.float32),
        grid_spec=pltpu.PrefetchScalarGridSpec(
            num_scalar_prefetch=1,
            grid=(steps,),
            in_specs=[
                pl.BlockSpec((rows, tile), lambda k, h: (h[0], k)),
                pl.BlockSpec((tile, ranks), lambda k, h: (k, 0)),
            ],
            out_specs=pl.BlockSpec((rows, ranks), lambda k, h: (0, 0)),
        ),
        compiler_params=params(),
        cost_estimate=pl.CostEstimate(
            flops=2 * rows * depth * ranks,
            bytes_accessed=2 * (rows * depth + depth * ranks) + 4 * rows * ranks,
            transcendentals=0,
        ),
        name="rank_half",
    )(half, activations, basis)


def partial_sums(place, grads, grads_got, rank_own, rank_got):
    tokens, ranks = rank_own.shape
    owned = grads_got.shape[1] // 2

    def kernel(place_ref, g_ref, got_ref, t_ref, u_ref, send_ref, keep_ref):
        dims = (((0,), (0,)), ((), ()))
        total = lax.dot_general(
            g_ref[...], t_ref[...], dims, preferred_element_type=jnp.float32
        ) + lax.dot_general(got_ref[...], u_ref[...], dims, preferred_element_type=jnp.float32)

        @pl.when(pl.program_id(0) == 0)
        def _():
            send_ref[...] = total.astype(send_ref.dtype)

        @pl.when(pl.program_id(0) == 1)
        def _():
            keep_ref[...] = total

    def side(i, p):
        return lax.rem(p[1] + 1 + i, 2)

    whole = pl.BlockSpec((tokens, ranks), lambda i, p: (0, 0))
    return pl.pallas_call(
        kernel,
        out_shape=(
            jax.ShapeDtypeStruct((owned, ranks), jnp.bfloat16),
            jax.ShapeDtypeStruct((owned, ranks), jnp.float32),
        ),
        grid_spec=pltpu.PrefetchScalarGridSpec(
            num_scalar_prefetch=1,
            grid=(2,),
            in_specs=[
                pl.BlockSpec((tokens, owned), lambda i, p: (0, p[0] + side(i, p))),
                pl.BlockSpec((tokens, owned), lambda i, p: (0, side(i, p))),
                whole,
                whole,
            ],
            out_specs=(
                pl.BlockSpec((owned, ranks), lambda i, p: (0, 0)),
                pl.BlockSpec((owned, ranks), lambda i, p: (0, 0)),
            ),
        ),
        compiler_params=params(),
        cost_estimate=pl.CostEstimate(
            flops=2 * 2 * tokens * 2 * owned * ranks,
            bytes_accessed=2 * 2 * tokens * (2 * owned + ranks) + 6 * owned * ranks,
            transcendentals=0,
        ),
        name="partial_sums",
    )(place, grads, grads_got, rank_own, rank_got)


def update_rows(group, normed, basis, groups, before=None, steps=4):
    owned, ranks = normed.shape
    width = basis.shape[0]
    tile = width // steps

    def kernel(group_ref, n_ref, b_ref, *refs):
        refs[-1][0] = lax.dot_general(
            n_ref[...], b_ref[...], (((1,), (1,)), ((), ())), preferred_element_type=jnp.float32
        ).astype(jnp.bfloat16)

    more = () if before is None else (before,)
    return pl.pallas_call(
        kernel,
        out_shape=jax.ShapeDtypeStruct((groups, owned, width), jnp.bfloat16),
        grid_spec=pltpu.PrefetchScalarGridSpec(
            num_scalar_prefetch=1,
            grid=(steps,),
            in_specs=[
                pl.BlockSpec((owned, ranks), lambda n, g: (0, 0)),
                pl.BlockSpec((tile, ranks), lambda n, g: (n, 0)),
            ]
            + [pl.BlockSpec(memory_space=pl.ANY) for _ in more],
            out_specs=pl.BlockSpec((1, owned, tile), lambda n, g: (g[0], 0, n)),
        ),
        input_output_aliases={3: 0} if more else {},
        compiler_params=params(),
        cost_estimate=pl.CostEstimate(
            flops=2 * owned * ranks * width,
            bytes_accessed=2 * (owned * ranks + width * ranks + owned * width),
            transcendentals=0,
        ),
        name="update_rows",
    )(group, normed, basis, *more)


def staged(activations, out_grads, basis, moment1, moment2):
    shards = lax.axis_size("dp")
    planes = shards // 4
    owned = moment1.shape[0]
    me, core = lax.axis_index("dp"), lax.axis_index("mp")
    z, y, x = me // 4, me // 2 % 2, me % 2

    along_y = [(i, i ^ 2) for i in range(shards)]
    along_x = [(i, i ^ 1) for i in range(shards)]
    last = planes - 1
    outer = [(0, 1), (last, last - 1)]
    inner = [(1, 2), (2, 1)]
    to_end = [(1, 0), (2, last)]
    outer, inner, to_end = (
        [(4 * a + k, 4 * b + k) for a, b in hops for k in range(4)] for hops in (outer, inner, to_end)
    )
    cores = [(0, 1), (1, 0)]

    order = np.array(
        [
            sorted(
                range(planes),
                key=lambda d, p=p: (d == p, -abs(d - p), (d < p) == (p < planes // 2)),
            )
            for p in range(planes)
        ],
        np.int32,
    )
    blocks = jnp.asarray(order)[z]

    wide = 2 * owned
    got = []
    for c in range(planes):
        mine = lax.dynamic_slice_in_dim(out_grads, (blocks[c] * 4 + (1 - y) * 2) * owned, wide, 1)
        got.append(lax.ppermute(mine, "dp", along_y))

    other = rank_half((1 - core)[None].astype(jnp.int32), activations, basis)
    arrived = lax.ppermute(other, "mp", cores)
    own = rank_half(core[None].astype(jnp.int32), activations, basis)
    half = (own + arrived).astype(jnp.bfloat16)
    half_far = lax.ppermute(half, "dp", along_y)
    half_other = lax.ppermute(half, "mp", cores)
    half_far_other = lax.ppermute(half_far, "mp", cores)

    def joined(a, b):
        first = core == 0
        return jnp.concatenate([jnp.where(first, a, b), jnp.where(first, b, a)])

    rank_own, rank_got = joined(half, half_other), joined(half_far, half_far_other)

    sums = []
    for c in range(planes):
        place = jnp.stack([blocks[c] * 4 + y * 2, x]).astype(jnp.int32)
        send, keep = partial_sums(place, out_grads, got[c], rank_own, rank_got)
        sums.append(keep + lax.ppermute(send, "dp", along_x).astype(jnp.float32))

    def hop(value, pairs):
        return lax.ppermute(value.astype(jnp.bfloat16), "dp", pairs).astype(jnp.float32)

    first, second, third, final = sums
    out1 = hop(first, outer)
    out2 = hop(second, outer)
    in2 = hop(first + out1, inner)
    out3 = hop(third, outer)
    in3 = hop(second + out2, inner)
    end3 = hop(third + in2, to_end)
    reduced = final + out3 + in3 + end3

    new_first, new_second, normed = adam(reduced, moment1, moment2)
    normed_other = lax.ppermute(normed, "mp", cores)
    update = update_rows(core[None].astype(jnp.int32), normed, basis, 2)
    update = update_rows((1 - core)[None].astype(jnp.int32), normed_other, basis, 2, update)
    return new_first, new_second, update


def solution(mesh):
    fits = mesh.shape["mp"] == 2 and mesh.shape["dp"] == 16
    return jax.shard_map(
        staged if fits else plain,
        mesh=mesh,
        in_specs=(
            P("dp", "mp"),
            P("dp", "mp"),
            P("mp", None),
            P(("mp", "dp"), None),
            P(("mp", "dp"), None),
        ),
        out_specs=(P(("mp", "dp"), None), P(("mp", "dp"), None), P(None, "dp", "mp")),
        check_vma=False,
    )
```

```python
import jax
import jax.numpy as jnp
from jax import lax
from jax.experimental import pallas as pl
from jax.experimental.pallas import tpu as pltpu
from jax.sharding import PartitionSpec as P

STEP = 100


beta_first = 0.9
beta_second = 0.999
epsilon = 1e-08


def adam(reduced, moment1, moment2):
    new_first = beta_first * moment1 + (1.0 - beta_first) * reduced
    new_second = beta_second * moment2 + (1.0 - beta_second) * reduced * reduced
    bias_first = 1.0 - beta_first**STEP
    bias_second = 1.0 - beta_second**STEP
    normed = (new_first / bias_first / (jnp.sqrt(new_second / bias_second) + epsilon)).astype(
        jnp.bfloat16
    )
    return new_first, new_second, normed


def plain(activations, out_grads, basis, moment1, moment2):
    partial_rank = jnp.dot(activations, basis, preferred_element_type=jnp.float32)
    token_rank = lax.psum(partial_rank, "mp").astype(jnp.bfloat16)
    reduced = lax.psum_scatter(
        lax.dot_general(
            out_grads, token_rank, (((0,), (0,)), ((), ())), preferred_element_type=jnp.float32
        ),
        "dp",
        scatter_dimension=0,
        tiled=True,
    )
    new_first, new_second, normed = adam(reduced, moment1, moment2)
    gathered = lax.all_gather(normed[None], "mp", axis=0, tiled=True)
    groups, owned, ranks = gathered.shape
    full = lax.dot_general(
        gathered.reshape(groups * owned, ranks),
        basis,
        (((1,), (1,)), ((), ())),
        preferred_element_type=jnp.float32,
    )
    return new_first, new_second, full.astype(jnp.bfloat16).reshape(groups, owned, basis.shape[0])


def whole(rows, columns):
    return pl.BlockSpec((rows, columns), lambda *_: (0, 0))


def call(kernel, name, outs, specs, mib, flops, moved, out_specs=None, grid=(1,), scratch=()):
    return pl.pallas_call(
        kernel,
        out_shape=outs,
        grid_spec=pltpu.PrefetchScalarGridSpec(
            num_scalar_prefetch=1,
            grid=grid,
            in_specs=specs,
            out_specs=[whole(*o.shape) for o in outs] if out_specs is None else out_specs,
            scratch_shapes=scratch,
        ),
        compiler_params=pltpu.CompilerParams(vmem_limit_bytes=mib * 1024 * 1024),
        cost_estimate=pl.CostEstimate(flops=flops, bytes_accessed=moved, transcendentals=0),
        name=name,
    )


def shape(rows, columns, dtype):
    return jax.ShapeDtypeStruct((rows, columns), dtype)


def take(place, grads, pieces, wide):
    def kernel(place_ref, g_ref, *refs):
        outs, sems = refs[:-1], refs[-1]
        copies = []
        for k, ((entry, first, rows), out) in enumerate(zip(pieces, outs)):
            columns = pl.ds(pl.multiple_of(place_ref[entry] * wide, wide), wide)
            copies.append(
                pltpu.make_async_copy(g_ref.at[pl.ds(first, rows), columns], out, sems.at[k])
            )
        for copy in copies:
            copy.start()
        for copy in copies:
            copy.wait()

    outs = [shape(rows, wide, grads.dtype) for _, _, rows in pieces]
    return call(
        kernel,
        "take",
        outs,
        [pl.BlockSpec(memory_space=pl.ANY)],
        8,
        0,
        4 * wide * sum(rows for _, _, rows in pieces),
        scratch=[pltpu.SemaphoreType.DMA((len(pieces),))],
    )(place, grads)


def rank_halves(place, activations, basis, core_at, steps=4):
    tokens, depth = activations.shape
    ranks = basis.shape[1] // 2
    tile = depth // steps

    def kernel(place_ref, a_ref, b_ref, other_ref, own_ref):
        core = place_ref[core_at]
        for o_ref, half in ((other_ref, 1 - core), (own_ref, core)):
            columns = pl.ds(pl.multiple_of(half * ranks, ranks), ranks)
            part = jnp.dot(a_ref[...], b_ref[:, columns], preferred_element_type=jnp.float32)

            @pl.when(pl.program_id(0) == 0)
            def _():
                o_ref[...] = part

            @pl.when(pl.program_id(0) > 0)
            def _():
                o_ref[...] += part

    half = shape(tokens, ranks, jnp.float32)
    return call(
        kernel,
        "rank_halves",
        [half, half],
        [
            pl.BlockSpec((tokens, tile), lambda k, p: (0, k)),
            pl.BlockSpec((tile, 2 * ranks), lambda k, p: (k, 0)),
        ],
        16,
        4 * tokens * depth * ranks,
        2 * (tokens + 2 * ranks) * depth + 8 * tokens * ranks,
        grid=(steps,),
    )(place, activations, basis)


def added(place, terms, dtype, masked=(), mask_at=None):
    rows, columns = terms[0].shape
    count = len(terms)

    def kernel(place_ref, *refs):
        total = refs[0][...].astype(jnp.float32)
        for ref in refs[1:count]:
            total += ref[...].astype(jnp.float32)
        for ref in refs[count:-1]:
            total += jnp.where(place_ref[mask_at] == 1, ref[...].astype(jnp.float32), 0.0)
        refs[-1][...] = total.astype(dtype)

    operands = [*terms, *masked]
    return call(
        kernel,
        "added",
        [shape(rows, columns, dtype)],
        [whole(rows, columns)] * len(operands),
        12,
        rows * columns * len(operands),
        4 * rows * columns * len(operands),
    )(place, *operands)[0]


def partial_sums(place, grads, got, rank_own, rank_got, block_at, x_at):
    tokens, ranks = rank_own[0].shape
    wide = got[0].shape[1]
    owned = wide // 2
    pieces = len(got)

    def kernel(place_ref, g_ref, *refs):
        got_refs, (t0_ref, t1_ref, u0_ref, u1_ref, send_ref, keep_ref) = refs[:pieces], refs[pieces:]
        x = place_ref[x_at]
        theirs = pl.ds(pl.multiple_of((1 - x) * owned, owned), owned)
        ours = pl.ds(pl.multiple_of(x * owned, owned), owned)
        mine = jnp.concatenate([g_ref[:, theirs], g_ref[:, ours]], axis=1)
        far = jnp.concatenate(
            [jnp.concatenate([r[:, theirs], r[:, ours]], axis=1) for r in got_refs], axis=0
        )
        dims = (((0,), (0,)), ((), ()))
        for side, (t_ref, u_ref) in enumerate(((t0_ref, u0_ref), (t1_ref, u1_ref))):
            total = lax.dot_general(
                mine, t_ref[...], dims, preferred_element_type=jnp.float32
            ) + lax.dot_general(far, u_ref[...], dims, preferred_element_type=jnp.float32)
            columns = slice(side * ranks, (side + 1) * ranks)
            send_ref[:, columns] = total[:owned].astype(send_ref.dtype)
            keep_ref[:, columns] = total[owned:]

    return call(
        kernel,
        "partial_sums",
        [shape(owned, 2 * ranks, jnp.bfloat16), shape(owned, 2 * ranks, jnp.float32)],
        [pl.BlockSpec((tokens, wide), lambda i, p: (0, p[block_at]))]
        + [whole(*g.shape) for g in got]
        + [whole(tokens, ranks)] * 4,
        20,
        8 * tokens * wide * ranks,
        4 * tokens * (wide + 2 * ranks) + 12 * owned * ranks,
    )(place, grads, *got, *rank_own, *rank_got)


def moments(place, terms, masked, moment1, moment2, mask_at, core_at, steps=4):
    owned, ranks = moment1.shape
    rows = owned // steps
    count = len(terms)

    def kernel(place_ref, *refs):
        total = refs[0][...].astype(jnp.float32)
        for ref in refs[1:count]:
            total += ref[...].astype(jnp.float32)
        total += jnp.where(place_ref[mask_at] == 1, refs[count][...].astype(jnp.float32), 0.0)
        here, there = total[:, : ranks // 2], total[:, ranks // 2 :]
        first = place_ref[core_at] == 0
        reduced = jnp.concatenate(
            [jnp.where(first, here, there), jnp.where(first, there, here)], axis=1
        )
        m1_ref, m2_ref, first_ref, second_ref, normed_ref = refs[count + 1 :]
        first_ref[...], second_ref[...], normed_ref[...] = adam(reduced, m1_ref[...], m2_ref[...])

    block = pl.BlockSpec((rows, ranks), lambda i, p: (i, 0))
    wide = shape(owned, ranks, jnp.float32)
    return call(
        kernel,
        "moments",
        [wide, wide, shape(owned, ranks, jnp.bfloat16)],
        [block] * (count + 3),
        12,
        20 * owned * ranks,
        28 * owned * ranks,
        out_specs=[block] * 3,
        grid=(steps,),
    )(place, *terms, masked, moment1, moment2)


def update_rows(place, normed, normed_other, basis, core_at, steps=8):
    owned, ranks = normed.shape
    width = basis.shape[0]
    tile = width // steps

    def kernel(place_ref, n_ref, m_ref, b_ref, o_ref):
        core = place_ref[core_at]
        rows = jnp.concatenate([n_ref[...], m_ref[...]])
        here = pl.ds(pl.multiple_of(pl.program_id(0) * tile, tile), tile)
        full = lax.dot_general(
            rows, b_ref[here, :], (((1,), (1,)), ((), ())), preferred_element_type=jnp.float32
        ).astype(jnp.bfloat16)
        o_ref[core] = full[:owned]
        o_ref[1 - core] = full[owned:]

    return call(
        kernel,
        "update_rows",
        [jax.ShapeDtypeStruct((2, owned, width), jnp.bfloat16)],
        [whole(owned, ranks), whole(owned, ranks), pl.BlockSpec(memory_space=pltpu.VMEM)],
        16,
        4 * owned * ranks * width,
        2 * (2 * owned * ranks + width * ranks + 2 * owned * width),
        out_specs=[pl.BlockSpec((2, owned, tile), lambda n, p: (0, 0, n))],
        grid=(steps,),
    )(place, normed, normed_other, basis)[0]


def staged(activations, out_grads, basis, moment1, moment2):
    shards = lax.axis_size("dp")
    planes = shards // 4
    owned = moment1.shape[0]
    tokens = activations.shape[0]
    me, core = lax.axis_index("dp"), lax.axis_index("mp")
    z, y, x = me // 4, me // 2 % 2, me % 2
    mid = (z > 0) & (z < planes - 1)

    along_y = [(i, i ^ 2) for i in range(shards)]
    along_x = [(i, i ^ 1) for i in range(shards)]
    outer = [(i, i ^ 4) for i in range(shards)]
    inner = [(i, i ^ 12 if 4 <= i < shards - 4 else i) for i in range(shards)]
    cores = [(0, 1), (1, 0)]

    order = [
        sorted(
            range(planes),
            key=lambda d, p=p: (d == p, -abs(d - p), (d < p) == (p < planes // 2)),
        )
        for p in range(planes)
    ]
    blocks = [
        sum(jnp.where(z == p, order[p][c], 0) for p in range(planes)) for c in range(planes)
    ]
    place = jnp.stack(
        [b * 2 + 1 - y for b in blocks] + [b * 2 + y for b in blocks] + [x, core, mid]
    ).astype(jnp.int32)
    x_at, core_at, mid_at = range(2 * planes, 2 * planes + 3)

    wide = 2 * owned
    split = tokens * 3 // 4
    grads, basis_hbm = (pltpu.with_memory_space_constraint(a, pltpu.HBM) for a in (out_grads, basis))
    early, late = take(place, grads, [(0, 0, split), (0, split, tokens - split)], wide)
    activations, early, late = lax.optimization_barrier((activations, early, late))
    early = lax.ppermute(early, "dp", along_y)
    late = lax.ppermute(late, "dp", along_y)

    activations = pltpu.with_memory_space_constraint(activations, pltpu.HBM)
    other, own = rank_halves(place, activations, basis_hbm, core_at)
    other, own, early = lax.optimization_barrier((other, own, early))
    arrived = lax.ppermute(other, "mp", cores)
    own, late = lax.optimization_barrier((own, late))
    half = added(place, [own, arrived], jnp.bfloat16)
    half_far = lax.ppermute(half, "dp", along_y)
    half_other = lax.ppermute(half, "mp", cores)
    place_later, _ = lax.optimization_barrier((place, half))
    rest = take(place_later, grads, [(c, 0, tokens) for c in range(1, planes)], wide)
    half_far, *rest = lax.optimization_barrier((half_far, *rest))
    half_far_other = lax.ppermute(half_far, "mp", cores)
    rank_own, rank_got = (half, half_other), (half_far, half_far_other)
    got = [[early, late]] + [[lax.ppermute(mine, "dp", along_y)] for mine in rest]

    sums = []
    for c in range(planes):
        send, keep = partial_sums(
            place, grads, got[c], rank_own, rank_got, planes + c, x_at
        )
        sums.append([keep, lax.ppermute(send, "dp", along_x)])

    def hop(terms, pairs, *masked):
        return lax.ppermute(added(place, terms, jnp.bfloat16, masked, mid_at), "dp", pairs)

    first, second, third, final = sums
    out1 = hop(first, outer)
    out2 = hop(second, outer)
    in2 = hop([*first, out1], inner)
    out3 = hop(third, outer, in2)
    in3 = hop([*second, out2], inner)

    new_first, new_second, normed = moments(
        place, [*final, out3], in3, moment1, moment2, mid_at, core_at
    )
    normed_other = lax.ppermute(normed, "mp", cores)
    update = update_rows(place, normed, normed_other, basis, core_at)
    return new_first, new_second, update


def solution(mesh):
    fits = mesh.shape["mp"] == 2 and mesh.shape["dp"] == 16
    return jax.shard_map(
        staged if fits else plain,
        mesh=mesh,
        in_specs=(
            P("dp", "mp"),
            P("dp", "mp"),
            P("mp", None),
            P(("mp", "dp"), None),
            P(("mp", "dp"), None),
        ),
        out_specs=(P(("mp", "dp"), None), P(("mp", "dp"), None), P(None, "dp", "mp")),
        check_vma=False,
    )
```

```python
import jax
import jax.numpy as jnp
from jax import lax
from jax.experimental import pallas as pl
from jax.experimental.pallas import tpu as pltpu
from jax.sharding import PartitionSpec as P

STEP = 100


beta_first = 0.9
beta_second = 0.999
epsilon = 1e-08


def adam(reduced, moment1, moment2):
    new_first = beta_first * moment1 + (1.0 - beta_first) * reduced
    new_second = beta_second * moment2 + (1.0 - beta_second) * reduced * reduced
    bias_first = 1.0 - beta_first**STEP
    bias_second = 1.0 - beta_second**STEP
    normed = (new_first / bias_first / (jnp.sqrt(new_second / bias_second) + epsilon)).astype(
        jnp.bfloat16
    )
    return new_first, new_second, normed


def plain(activations, out_grads, basis, moment1, moment2):
    partial_rank = jnp.dot(activations, basis, preferred_element_type=jnp.float32)
    token_rank = lax.psum(partial_rank, "mp").astype(jnp.bfloat16)
    reduced = lax.psum_scatter(
        lax.dot_general(
            out_grads, token_rank, (((0,), (0,)), ((), ())), preferred_element_type=jnp.float32
        ),
        "dp",
        scatter_dimension=0,
        tiled=True,
    )
    new_first, new_second, normed = adam(reduced, moment1, moment2)
    gathered = lax.all_gather(normed[None], "mp", axis=0, tiled=True)
    groups, owned, ranks = gathered.shape
    full = lax.dot_general(
        gathered.reshape(groups * owned, ranks),
        basis,
        (((1,), (1,)), ((), ())),
        preferred_element_type=jnp.float32,
    )
    return new_first, new_second, full.astype(jnp.bfloat16).reshape(groups, owned, basis.shape[0])


def whole(rows, columns):
    return pl.BlockSpec((rows, columns), lambda *_: (0, 0))


def call(kernel, name, outs, specs, mib, flops, moved, out_specs=None, grid=(1,), scratch=()):
    return pl.pallas_call(
        kernel,
        out_shape=outs,
        grid_spec=pltpu.PrefetchScalarGridSpec(
            num_scalar_prefetch=1,
            grid=grid,
            in_specs=specs,
            out_specs=[whole(*o.shape) for o in outs] if out_specs is None else out_specs,
            scratch_shapes=scratch,
        ),
        compiler_params=pltpu.CompilerParams(vmem_limit_bytes=mib * 1024 * 1024),
        cost_estimate=pl.CostEstimate(flops=flops, bytes_accessed=moved, transcendentals=0),
        name=name,
    )


def shape(rows, columns, dtype):
    return jax.ShapeDtypeStruct((rows, columns), dtype)


def take(place, grads, pieces, wide):
    def kernel(place_ref, g_ref, *refs):
        outs, sems = refs[:-1], refs[-1]
        copies = []
        for k, ((entry, first, rows), out) in enumerate(zip(pieces, outs)):
            columns = pl.ds(pl.multiple_of(place_ref[entry] * wide, wide), wide)
            copies.append(
                pltpu.make_async_copy(g_ref.at[pl.ds(first, rows), columns], out, sems.at[k])
            )
        for copy in copies:
            copy.start()
        for copy in copies:
            copy.wait()

    outs = [shape(rows, wide, grads.dtype) for _, _, rows in pieces]
    return call(
        kernel,
        "take",
        outs,
        [pl.BlockSpec(memory_space=pl.ANY)],
        8,
        0,
        4 * wide * sum(rows for _, _, rows in pieces),
        scratch=[pltpu.SemaphoreType.DMA((len(pieces),))],
    )(place, grads)


def rank_halves(place, activations, basis, core_at, pieces=(1, 3, 4)):
    tokens, depth = activations.shape
    ranks = basis.shape[1] // 2
    unit = depth // sum(pieces)
    ends = [unit * sum(pieces[: k + 1]) for k in range(len(pieces))]
    spans = [slice(end - unit * n, end) for end, n in zip(ends, pieces)]

    def kernel(place_ref, a_hbm, b_hbm, other_ref, own_ref, a_ref, b_ref, total_ref, sems):
        core = place_ref[core_at]
        copies = []
        for k, span in enumerate(spans):
            copies.append(
                (
                    pltpu.make_async_copy(a_hbm.at[:, span], a_ref.at[:, span], sems.at[2 * k]),
                    pltpu.make_async_copy(b_hbm.at[span, :], b_ref.at[span, :], sems.at[2 * k + 1]),
                )
            )
        for pair in copies:
            for copy in pair:
                copy.start()
        for k, (span, pair) in enumerate(zip(spans, copies)):
            for copy in pair:
                copy.wait()
            for o_ref, half in ((total_ref, 1 - core), (own_ref, core)):
                columns = pl.ds(pl.multiple_of(half * ranks, ranks), ranks)
                part = jnp.dot(
                    a_ref[:, span], b_ref[span, columns], preferred_element_type=jnp.float32
                )
                if k:
                    part = o_ref[...] + part
                if k == len(spans) - 1 and o_ref is total_ref:
                    other_ref[...] = part.astype(other_ref.dtype)
                else:
                    o_ref[...] = part

    return call(
        kernel,
        "rank_halves",
        [shape(tokens, ranks, jnp.bfloat16), shape(tokens, ranks, jnp.float32)],
        [pl.BlockSpec(memory_space=pl.ANY)] * 2,
        24,
        4 * tokens * depth * ranks,
        2 * (tokens + 2 * ranks) * depth + 8 * tokens * ranks,
        scratch=[
            pltpu.VMEM((tokens, depth), activations.dtype),
            pltpu.VMEM((depth, 2 * ranks), basis.dtype),
            pltpu.VMEM((tokens, ranks), jnp.float32),
            pltpu.SemaphoreType.DMA((2 * len(pieces),)),
        ],
    )(place, activations, basis)


def added(place, terms, dtype, masked=(), mask_at=None):
    rows, columns = terms[0].shape
    count = len(terms)

    def kernel(place_ref, *refs):
        total = refs[0][...].astype(jnp.float32)
        for ref in refs[1:count]:
            total += ref[...].astype(jnp.float32)
        for ref in refs[count:-1]:
            total += jnp.where(place_ref[mask_at] == 1, ref[...].astype(jnp.float32), 0.0)
        refs[-1][...] = total.astype(dtype)

    operands = [*terms, *masked]
    return call(
        kernel,
        "added",
        [shape(rows, columns, dtype)],
        [whole(rows, columns)] * len(operands),
        12,
        rows * columns * len(operands),
        4 * rows * columns * len(operands),
    )(place, *operands)[0]


def partial_sums(place, grads, got, rank_own, rank_got, block_at, x_at):
    tokens, ranks = rank_own[0].shape
    wide = got[0].shape[1]
    owned = wide // 2
    pieces = len(got)

    def kernel(place_ref, g_ref, *refs):
        got_refs, (t0_ref, t1_ref, u0_ref, u1_ref, send_ref, keep_ref) = refs[:pieces], refs[pieces:]
        x = place_ref[x_at]
        theirs = pl.ds(pl.multiple_of((1 - x) * owned, owned), owned)
        ours = pl.ds(pl.multiple_of(x * owned, owned), owned)
        mine = jnp.concatenate([g_ref[:, theirs], g_ref[:, ours]], axis=1)
        far = jnp.concatenate(
            [jnp.concatenate([r[:, theirs], r[:, ours]], axis=1) for r in got_refs], axis=0
        )
        dims = (((0,), (0,)), ((), ()))
        for side, (t_ref, u_ref) in enumerate(((t0_ref, u0_ref), (t1_ref, u1_ref))):
            total = lax.dot_general(
                mine, t_ref[...], dims, preferred_element_type=jnp.float32
            ) + lax.dot_general(far, u_ref[...], dims, preferred_element_type=jnp.float32)
            columns = slice(side * ranks, (side + 1) * ranks)
            send_ref[:, columns] = total[:owned].astype(send_ref.dtype)
            keep_ref[:, columns] = total[owned:]

    return call(
        kernel,
        "partial_sums",
        [shape(owned, 2 * ranks, jnp.bfloat16), shape(owned, 2 * ranks, jnp.float32)],
        [pl.BlockSpec((tokens, wide), lambda i, p: (0, p[block_at]))]
        + [whole(*g.shape) for g in got]
        + [whole(tokens, ranks)] * 4,
        20,
        8 * tokens * wide * ranks,
        4 * tokens * (wide + 2 * ranks) + 12 * owned * ranks,
    )(place, grads, *got, *rank_own, *rank_got)


def moments(place, terms, masked, moment1, moment2, mask_at, core_at, steps=2):
    owned, ranks = moment1.shape
    rows = owned // steps
    count = len(terms)

    def kernel(place_ref, *refs):
        total = refs[0][...].astype(jnp.float32)
        for ref in refs[1:count]:
            total += ref[...].astype(jnp.float32)
        total += jnp.where(place_ref[mask_at] == 1, refs[count][...].astype(jnp.float32), 0.0)
        here, there = total[:, : ranks // 2], total[:, ranks // 2 :]
        first = place_ref[core_at] == 0
        reduced = jnp.concatenate(
            [jnp.where(first, here, there), jnp.where(first, there, here)], axis=1
        )
        m1_ref, m2_ref, first_ref, second_ref, normed_ref = refs[count + 1 :]
        first_ref[...], second_ref[...], normed_ref[...] = adam(reduced, m1_ref[...], m2_ref[...])

    block = pl.BlockSpec((rows, ranks), lambda i, p: (i, 0))
    wide = shape(owned, ranks, jnp.float32)
    return call(
        kernel,
        "moments",
        [wide, wide, shape(owned, ranks, jnp.bfloat16)],
        [block] * (count + 3),
        12,
        20 * owned * ranks,
        28 * owned * ranks,
        out_specs=[block] * 3,
        grid=(steps,),
    )(place, *terms, masked, moment1, moment2)


def update_rows(place, normed, normed_other, basis, core_at, steps=4):
    owned, ranks = normed.shape
    width = basis.shape[0]
    tile = width // steps

    def kernel(place_ref, n_ref, m_ref, b_ref, o_ref):
        core = place_ref[core_at]
        rows = jnp.concatenate([n_ref[...], m_ref[...]])
        here = pl.ds(pl.multiple_of(pl.program_id(0) * tile, tile), tile)
        full = lax.dot_general(
            rows, b_ref[here, :], (((1,), (1,)), ((), ())), preferred_element_type=jnp.float32
        ).astype(jnp.bfloat16)
        o_ref[core] = full[:owned]
        o_ref[1 - core] = full[owned:]

    return call(
        kernel,
        "update_rows",
        [jax.ShapeDtypeStruct((2, owned, width), jnp.bfloat16)],
        [whole(owned, ranks), whole(owned, ranks), pl.BlockSpec(memory_space=pltpu.VMEM)],
        16,
        4 * owned * ranks * width,
        2 * (2 * owned * ranks + width * ranks + 2 * owned * width),
        out_specs=[pl.BlockSpec((2, owned, tile), lambda n, p: (0, 0, n))],
        grid=(steps,),
    )(place, normed, normed_other, basis)[0]


def staged(activations, out_grads, basis, moment1, moment2):
    shards = lax.axis_size("dp")
    planes = shards // 4
    owned = moment1.shape[0]
    tokens = activations.shape[0]
    me, core = lax.axis_index("dp"), lax.axis_index("mp")
    z, y, x = me // 4, me // 2 % 2, me % 2
    mid = (z > 0) & (z < planes - 1)

    along_y = [(i, i ^ 2) for i in range(shards)]
    along_x = [(i, i ^ 1) for i in range(shards)]
    outer = [(i, i ^ 4) for i in range(shards)]
    inner = [
        (2 * i + k, 2 * (i ^ 12) + k if 4 <= i < shards - 4 else 2 * i + 1 - k)
        for i in range(shards)
        for k in range(2)
    ]
    cores = [(0, 1), (1, 0)]

    order = [
        sorted(
            range(planes),
            key=lambda d, p=p: (d == p, -abs(d - p), (d < p) == (p < planes // 2)),
        )
        for p in range(planes)
    ]
    blocks = [
        sum(jnp.where(z == p, order[p][c], 0) for p in range(planes)) for c in range(planes)
    ]
    place = jnp.stack(
        [b * 2 + 1 - y for b in blocks] + [b * 2 + y for b in blocks] + [x, core, mid]
    ).astype(jnp.int32)
    x_at, core_at, mid_at = range(2 * planes, 2 * planes + 3)

    wide = 2 * owned
    grads, basis_hbm = (pltpu.with_memory_space_constraint(a, pltpu.HBM) for a in (out_grads, basis))
    (mine,) = take(place, grads, [(0, 0, tokens)], wide)
    activations, mine = lax.optimization_barrier((activations, mine))
    near = lax.ppermute(mine, "dp", along_y)

    activations = pltpu.with_memory_space_constraint(activations, pltpu.HBM)
    other, own = rank_halves(place, activations, basis_hbm, core_at)
    other, own, near = lax.optimization_barrier((other, own, near))
    arrived = lax.ppermute(other, "mp", cores)
    half = added(place, [own, arrived], jnp.bfloat16)
    half_far = lax.ppermute(half, "dp", along_y)
    half_other = lax.ppermute(half, "mp", cores)
    place_later, _ = lax.optimization_barrier((place, half))
    rest = take(place_later, grads, [(c, 0, tokens) for c in range(1, planes)], wide)
    half_far, *rest = lax.optimization_barrier((half_far, *rest))
    half_far_other = lax.ppermute(half_far, "mp", cores)
    rank_own, rank_got = (half, half_other), (half_far, half_far_other)
    got = [[near]] + [[lax.ppermute(mine, "dp", along_y)] for mine in rest]

    sums = []
    for c in range(planes):
        send, keep = partial_sums(
            place, grads, got[c], rank_own, rank_got, planes + c, x_at
        )
        sums.append([keep, lax.ppermute(send, "dp", along_x)])

    def hop(terms, axes, pairs, *masked):
        return lax.ppermute(added(place, terms, jnp.bfloat16, masked, mid_at), axes, pairs)

    first, second, third, final = sums
    out1 = hop(first, "dp", outer)
    out2 = hop(second, "dp", outer)
    in2 = hop([*first, out1], ("dp", "mp"), inner)
    out3 = hop(third, "dp", outer, in2)
    place, _ = lax.optimization_barrier((place, third[1]))
    in3 = hop([*second, out2], ("dp", "mp"), inner)

    new_first, new_second, normed = moments(
        place, [*final, out3], in3, moment1, moment2, mid_at, core_at
    )
    normed_other = lax.ppermute(normed, "mp", cores)
    update = update_rows(place, normed, normed_other, basis, core_at)
    return new_first, new_second, update


def solution(mesh):
    fits = mesh.shape["mp"] == 2 and mesh.shape["dp"] == 16
    return jax.shard_map(
        staged if fits else plain,
        mesh=mesh,
        in_specs=(
            P("dp", "mp"),
            P("dp", "mp"),
            P("mp", None),
            P(("mp", "dp"), None),
            P(("mp", "dp"), None),
        ),
        out_specs=(P(("mp", "dp"), None), P(("mp", "dp"), None), P(None, "dp", "mp")),
        check_vma=False,
    )
```

```python
import jax
import jax.numpy as jnp
from jax import lax
from jax.experimental import pallas as pl
from jax.experimental.pallas import tpu as pltpu
from jax.sharding import PartitionSpec as P

STEP = 100


beta_first = 0.9
beta_second = 0.999
epsilon = 1e-08


def adam(reduced, moment1, moment2):
    new_first = beta_first * moment1 + (1.0 - beta_first) * reduced
    new_second = beta_second * moment2 + (1.0 - beta_second) * reduced * reduced
    bias_first = 1.0 - beta_first**STEP
    bias_second = 1.0 - beta_second**STEP
    normed = (new_first / bias_first / (jnp.sqrt(new_second / bias_second) + epsilon)).astype(
        jnp.bfloat16
    )
    return new_first, new_second, normed


def plain(activations, out_grads, basis, moment1, moment2):
    partial_rank = jnp.dot(activations, basis, preferred_element_type=jnp.float32)
    token_rank = lax.psum(partial_rank, "mp").astype(jnp.bfloat16)
    reduced = lax.psum_scatter(
        lax.dot_general(
            out_grads, token_rank, (((0,), (0,)), ((), ())), preferred_element_type=jnp.float32
        ),
        "dp",
        scatter_dimension=0,
        tiled=True,
    )
    new_first, new_second, normed = adam(reduced, moment1, moment2)
    gathered = lax.all_gather(normed[None], "mp", axis=0, tiled=True)
    groups, owned, ranks = gathered.shape
    full = lax.dot_general(
        gathered.reshape(groups * owned, ranks),
        basis,
        (((1,), (1,)), ((), ())),
        preferred_element_type=jnp.float32,
    )
    return new_first, new_second, full.astype(jnp.bfloat16).reshape(groups, owned, basis.shape[0])


def whole(rows, columns):
    return pl.BlockSpec((rows, columns), lambda *_: (0, 0))


def call(
    kernel, name, outs, specs, mib, flops, moved, out_specs=None, grid=(1,), scratch=(), aliases=None
):
    return pl.pallas_call(
        kernel,
        out_shape=outs,
        grid_spec=pltpu.PrefetchScalarGridSpec(
            num_scalar_prefetch=1,
            grid=grid,
            in_specs=specs,
            out_specs=[whole(*o.shape) for o in outs] if out_specs is None else out_specs,
            scratch_shapes=scratch,
        ),
        input_output_aliases=aliases or {},
        compiler_params=pltpu.CompilerParams(vmem_limit_bytes=mib * 1024 * 1024),
        cost_estimate=pl.CostEstimate(flops=flops, bytes_accessed=moved, transcendentals=0),
        name=name,
    )


def part(rows, columns, at):
    return pl.BlockSpec((rows, columns), lambda *_: (at, 0))


def shape(rows, columns, dtype):
    return jax.ShapeDtypeStruct((rows, columns), dtype)


def take(place, grads, pieces, owned):
    def kernel(place_ref, g_ref, *refs):
        outs, sems = refs[:-1], refs[-1]
        copies = []
        for k, ((entry, stride, first, rows), out) in enumerate(zip(pieces, outs)):
            for side in range(2):
                block = (place_ref[entry] + side * stride) * owned
                copies.append(
                    pltpu.make_async_copy(
                        g_ref.at[pl.ds(first, rows), pl.ds(pl.multiple_of(block, owned), owned)],
                        out.at[:, pl.ds(side * owned, owned)],
                        sems.at[2 * k + side],
                    )
                )
        for copy in copies:
            copy.start()
        for copy in copies:
            copy.wait()

    outs = [shape(rows, 2 * owned, grads.dtype) for _, _, _, rows in pieces]
    return call(
        kernel,
        "take",
        outs,
        [pl.BlockSpec(memory_space=pl.ANY)],
        8,
        0,
        8 * owned * sum(rows for _, _, _, rows in pieces),
        scratch=[pltpu.SemaphoreType.DMA((2 * len(pieces),))],
    )(place, grads)


def rank_halves(place, activations, basis, core_at, pieces=(1, 3, 4)):
    tokens, depth = activations.shape
    ranks = basis.shape[1] // 2
    unit = depth // sum(pieces)
    ends = [unit * sum(pieces[: k + 1]) for k in range(len(pieces))]
    spans = [slice(end - unit * n, end) for end, n in zip(ends, pieces)]

    def kernel(place_ref, a_hbm, b_hbm, other_ref, own_ref, a_ref, b_ref, total_ref, sems):
        core = place_ref[core_at]
        copies = []
        for k, span in enumerate(spans):
            copies.append(
                (
                    pltpu.make_async_copy(a_hbm.at[:, span], a_ref.at[:, span], sems.at[2 * k]),
                    pltpu.make_async_copy(b_hbm.at[span, :], b_ref.at[span, :], sems.at[2 * k + 1]),
                )
            )
        for pair in copies:
            for copy in pair:
                copy.start()
        for k, (span, pair) in enumerate(zip(spans, copies)):
            for copy in pair:
                copy.wait()
            for o_ref, half in ((total_ref, 1 - core), (own_ref, core)):
                columns = pl.ds(pl.multiple_of(half * ranks, ranks), ranks)
                part = jnp.dot(
                    a_ref[:, span], b_ref[span, columns], preferred_element_type=jnp.float32
                )
                if k:
                    part = o_ref[...] + part
                if k == len(spans) - 1 and o_ref is total_ref:
                    other_ref[...] = part.astype(other_ref.dtype)
                else:
                    o_ref[...] = part

    return call(
        kernel,
        "rank_halves",
        [shape(tokens, ranks, jnp.bfloat16), shape(tokens, ranks, jnp.float32)],
        [pl.BlockSpec(memory_space=pl.ANY)] * 2,
        24,
        4 * tokens * depth * ranks,
        2 * (tokens + 2 * ranks) * depth + 8 * tokens * ranks,
        scratch=[
            pltpu.VMEM((tokens, depth), activations.dtype),
            pltpu.VMEM((depth, 2 * ranks), basis.dtype),
            pltpu.VMEM((tokens, ranks), jnp.float32),
            pltpu.SemaphoreType.DMA((2 * len(pieces),)),
        ],
    )(place, activations, basis)


def added(place, keep, at, parts, terms, masked, mask_at):
    rows, ranks = keep.shape[0] // parts, keep.shape[1]
    operands = [*terms, *masked]
    pieces = max([len(term) for term in operands])
    height = rows // pieces
    flat = [piece for term in operands for piece in term]

    def kernel(place_ref, keep_ref, *refs):
        for k in range(pieces):
            here = slice(k * height, (k + 1) * height)
            total, first = keep_ref[here, :], 0
            for number, term in enumerate(operands):
                own = refs[first : first + len(term)]
                first += len(term)
                value = own[k][...] if len(term) == pieces else own[0][here, :]
                value = value.astype(jnp.float32)
                if number >= len(terms):
                    value = jnp.where(place_ref[mask_at] == 1, value, 0.0)
                total = total + value
            refs[-1][here, :] = total.astype(jnp.bfloat16)

    return call(
        kernel,
        "added",
        [shape(rows, ranks, jnp.bfloat16)],
        [part(rows, ranks, at)] + [whole(*piece.shape) for piece in flat],
        12,
        rows * ranks * len(operands),
        4 * rows * ranks * len(operands),
    )(place, keep, *flat)[0]


def rounded(place, own, arrived):
    def kernel(place_ref, a_ref, b_ref, o_ref):
        o_ref[...] = (a_ref[...] + b_ref[...].astype(jnp.float32)).astype(jnp.bfloat16)

    rows, columns = own.shape
    return call(
        kernel,
        "rounded",
        [shape(rows, columns, jnp.bfloat16)],
        [whole(rows, columns)] * 2,
        12,
        rows * columns,
        10 * rows * columns,
    )(place, own, arrived)[0]


def partial_sums(place, grads, got, rank_own, rank_got, theirs_at, ours_at, side_at, parts):
    tokens, ranks = rank_own[0].shape
    wide = got[0].shape[1]
    owned = wide // 2
    pieces = len(got)
    rows = owned // parts

    def kernel(place_ref, theirs_ref, ours_ref, *refs):
        got_refs, (t0_ref, t1_ref, u0_ref, u1_ref, *send_refs, keep_ref) = refs[:pieces], refs[pieces:]
        mine = jnp.concatenate([theirs_ref[...], ours_ref[...]], axis=1)
        near = place_ref[side_at]
        theirs = pl.ds(pl.multiple_of((1 - near) * owned, owned), owned)
        ours = pl.ds(pl.multiple_of(near * owned, owned), owned)
        far = jnp.concatenate(
            [jnp.concatenate([r[:, theirs], r[:, ours]], axis=1) for r in got_refs], axis=0
        )
        dims = (((0,), (0,)), ((), ()))
        for side, (t_ref, u_ref) in enumerate(((t0_ref, u0_ref), (t1_ref, u1_ref))):
            total = lax.dot_general(
                mine, t_ref[...], dims, preferred_element_type=jnp.float32
            ) + lax.dot_general(far, u_ref[...], dims, preferred_element_type=jnp.float32)
            columns = slice(side * ranks, (side + 1) * ranks)
            for at, send_ref in enumerate(send_refs):
                send_ref[:, columns] = total[at * rows : (at + 1) * rows].astype(send_ref.dtype)
            keep_ref[:, columns] = total[owned:]

    return call(
        kernel,
        "partial_sums",
        [shape(rows, 2 * ranks, jnp.bfloat16)] * parts + [shape(owned, 2 * ranks, jnp.float32)],
        [
            pl.BlockSpec((tokens, owned), lambda i, p: (0, p[theirs_at])),
            pl.BlockSpec((tokens, owned), lambda i, p: (0, p[ours_at])),
        ]
        + [whole(*g.shape) for g in got]
        + [whole(tokens, ranks)] * 4,
        20,
        8 * tokens * wide * ranks,
        4 * tokens * (wide + 2 * ranks) + 12 * owned * ranks,
    )(place, grads, grads, *got, *rank_own, *rank_got)


def moments(place, terms, masked, moment1, moment2, mask_at, core_at, steps=2):
    owned, ranks = moment1.shape
    rows = owned // steps
    count = len(terms)

    def kernel(place_ref, *refs):
        total = refs[0][...].astype(jnp.float32)
        for ref in refs[1:count]:
            total += ref[...].astype(jnp.float32)
        total += jnp.where(place_ref[mask_at] == 1, refs[count][...].astype(jnp.float32), 0.0)
        here, there = total[:, : ranks // 2], total[:, ranks // 2 :]
        first = place_ref[core_at] == 0
        reduced = jnp.concatenate(
            [jnp.where(first, here, there), jnp.where(first, there, here)], axis=1
        )
        m1_ref, m2_ref, first_ref, second_ref, normed_ref = refs[count + 1 :]
        first_ref[...], second_ref[...], normed_ref[...] = adam(reduced, m1_ref[...], m2_ref[...])

    block = pl.BlockSpec((rows, ranks), lambda i, p: (i, 0))
    wide = shape(owned, ranks, jnp.float32)
    return call(
        kernel,
        "moments",
        [wide, wide, shape(owned, ranks, jnp.bfloat16)],
        [block] * (count + 3),
        12,
        20 * owned * ranks,
        28 * owned * ranks,
        out_specs=[block] * 3,
        grid=(steps,),
    )(place, *terms, masked, moment1, moment2)


def update_rows(place, normed, normed_other, basis, core_at, steps=4):
    owned, ranks = normed.shape
    width = basis.shape[0]
    tile = width // steps

    def kernel(place_ref, n_ref, m_ref, b_ref, o_ref):
        core = place_ref[core_at]
        rows = jnp.concatenate([n_ref[...], m_ref[...]])
        here = pl.ds(pl.multiple_of(pl.program_id(0) * tile, tile), tile)
        full = lax.dot_general(
            rows, b_ref[here, :], (((1,), (1,)), ((), ())), preferred_element_type=jnp.float32
        ).astype(jnp.bfloat16)
        o_ref[core] = full[:owned]
        o_ref[1 - core] = full[owned:]

    return call(
        kernel,
        "update_rows",
        [jax.ShapeDtypeStruct((2, owned, width), jnp.bfloat16)],
        [whole(owned, ranks), whole(owned, ranks), pl.BlockSpec(memory_space=pltpu.VMEM)],
        16,
        4 * owned * ranks * width,
        2 * (2 * owned * ranks + width * ranks + 2 * owned * width),
        out_specs=[pl.BlockSpec((2, owned, tile), lambda n, p: (0, 0, n))],
        grid=(steps,),
    )(place, normed, normed_other, basis)[0]


def staged(activations, out_grads, basis, moment1, moment2):
    shards = lax.axis_size("dp")
    planes = shards // 4
    owned = moment1.shape[0]
    tokens = activations.shape[0]
    me, core = lax.axis_index("dp"), lax.axis_index("mp")
    z, y, x = me // 4, me // 2 % 2, me % 2
    mid = (z > 0) & (z < planes - 1)

    along_y = [(i, i ^ 2) for i in range(shards)]
    along_x = [(i, i ^ 1) for i in range(shards)]
    outer = [(i, i ^ 4) for i in range(shards)]
    inner = [
        (2 * i + k, 2 * (i ^ 12) + k if 4 <= i < shards - 4 else 2 * i + 1 - k)
        for i in range(shards)
        for k in range(2)
    ]
    cores = [(0, 1), (1, 0)]

    order = [
        sorted(
            range(planes),
            key=lambda d, p=p: (d == p, -abs(d - p), (d < p) == (p < planes // 2)),
        )
        for p in range(planes)
    ]
    blocks = [
        sum(jnp.where(z == p, order[p][c], 0) for p in range(planes)) for c in range(planes)
    ]
    first_y = [c != 1 for c in range(planes)]
    base = [b * 4 + ((1 - y) * 2 if f else 1 - x) for b, f in zip(blocks, first_y)]
    ours = [b * 4 + y * 2 + x for b in blocks]
    theirs = [b * 4 + (y * 2 + 1 - x if f else (1 - y) * 2 + x) for b, f in zip(blocks, first_y)]
    place = jnp.stack([*base, *ours, *theirs, x, y, core, mid]).astype(jnp.int32)
    ours_at, theirs_at = planes, 2 * planes
    x_at, y_at, core_at, mid_at = range(3 * planes, 3 * planes + 4)

    def piece(c, first=0, rows=tokens):
        return c, 1 if first_y[c] else 2, first, rows

    def raw(c, mine):
        return lax.ppermute(mine, "dp", along_y if first_y[c] else along_x)

    grads, basis_hbm = (pltpu.with_memory_space_constraint(a, pltpu.HBM) for a in (out_grads, basis))
    early = take(place, grads, [piece(0), piece(1)], owned)
    activations, *early = lax.optimization_barrier((activations, *early))
    first, second = (raw(c, mine) for c, mine in enumerate(early))

    activations = pltpu.with_memory_space_constraint(activations, pltpu.HBM)
    other, own = rank_halves(place, activations, basis_hbm, core_at)
    other, own, first, second = lax.optimization_barrier((other, own, first, second))
    arrived = lax.ppermute(other, "mp", cores)
    half = rounded(place, own, arrived)
    half_y = lax.ppermute(half, "dp", along_y)
    half_x = lax.ppermute(half, "dp", along_x)
    half_other = lax.ppermute(half, "mp", cores)
    place_later, _ = lax.optimization_barrier((place, half))
    rest = take(place_later, grads, [piece(c) for c in range(2, planes)], owned)
    half_y, *rest = lax.optimization_barrier((half_y, *rest))
    got = [[first], [second]] + [
        [raw(c, mine)] for c, mine in enumerate(rest, 2)
    ]
    rank_own = (half, half_other)
    rank_y = (half_y, lax.ppermute(half_y, "mp", cores))
    rank_x = (half_x, lax.ppermute(half_x, "mp", cores))

    parts = [2, 1, 1, 1]
    keeps, arrivals, now = {}, {}, [place]

    def then(result):
        return result

    def block(c):
        *sends, keeps[c] = then(
            partial_sums(
                now[0],
                grads,
                got[c],
                rank_own,
                rank_y if first_y[c] else rank_x,
                theirs_at + c,
                ours_at + c,
                x_at if first_y[c] else y_at,
                parts[c],
            )
        )
        second = along_x if first_y[c] else along_y
        arrivals[c] = [lax.ppermute(send, "dp", second) for send in sends]

    def hop(c, at, of, axes, pairs, terms=(), masked=()):
        come = arrivals[c] if of == 1 else [arrivals[c][at]]
        value = then(added(now[0], keeps[c], at, of, [come, *terms], masked, mid_at))
        return lax.ppermute(value, axes, pairs)

    both = ("dp", "mp")
    block(0)
    block(1)
    out1 = [hop(0, at, parts[0], "dp", outer) for at in range(parts[0])]
    block(2)
    in2 = hop(0, 0, 1, both, inner, [out1])
    out2 = hop(1, 0, 1, "dp", outer)
    block(3)
    out3 = hop(2, 0, 1, "dp", outer, masked=[[in2]])
    in3 = hop(1, 0, 1, both, inner, [[out2]])
    new_first, new_second, normed = moments(
        now[0], [keeps[3], *arrivals[3], out3], in3, moment1, moment2, mid_at, core_at
    )
    normed_other = lax.ppermute(normed, "mp", cores)
    update = update_rows(place, normed, normed_other, basis, core_at)
    return new_first, new_second, update


def solution(mesh):
    fits = mesh.shape["mp"] == 2 and mesh.shape["dp"] == 16
    return jax.shard_map(
        staged if fits else plain,
        mesh=mesh,
        in_specs=(
            P("dp", "mp"),
            P("dp", "mp"),
            P("mp", None),
            P(("mp", "dp"), None),
            P(("mp", "dp"), None),
        ),
        out_specs=(P(("mp", "dp"), None), P(("mp", "dp"), None), P(None, "dp", "mp")),
        check_vma=False,
    )
```

```python
import jax
import jax.numpy as jnp
from jax import lax
from jax.experimental import pallas as pl
from jax.experimental.pallas import tpu as pltpu
from jax.sharding import PartitionSpec as P

STEP = 100


beta_first = 0.9
beta_second = 0.999
epsilon = 1e-08


def adam(reduced, moment1, moment2):
    new_first = beta_first * moment1 + (1.0 - beta_first) * reduced
    new_second = beta_second * moment2 + (1.0 - beta_second) * reduced * reduced
    bias_first = 1.0 - beta_first**STEP
    bias_second = 1.0 - beta_second**STEP
    normed = (new_first / bias_first / (jnp.sqrt(new_second / bias_second) + epsilon)).astype(
        jnp.bfloat16
    )
    return new_first, new_second, normed


def plain(activations, out_grads, basis, moment1, moment2):
    partial_rank = jnp.dot(activations, basis, preferred_element_type=jnp.float32)
    token_rank = lax.psum(partial_rank, "mp").astype(jnp.bfloat16)
    reduced = lax.psum_scatter(
        lax.dot_general(
            out_grads, token_rank, (((0,), (0,)), ((), ())), preferred_element_type=jnp.float32
        ),
        "dp",
        scatter_dimension=0,
        tiled=True,
    )
    new_first, new_second, normed = adam(reduced, moment1, moment2)
    gathered = lax.all_gather(normed[None], "mp", axis=0, tiled=True)
    groups, owned, ranks = gathered.shape
    full = lax.dot_general(
        gathered.reshape(groups * owned, ranks),
        basis,
        (((1,), (1,)), ((), ())),
        preferred_element_type=jnp.float32,
    )
    return new_first, new_second, full.astype(jnp.bfloat16).reshape(groups, owned, basis.shape[0])


def whole(rows, columns):
    return pl.BlockSpec((rows, columns), lambda *_: (0, 0))


def call(
    kernel, name, outs, specs, mib, flops, moved, out_specs=None, grid=(1,), scratch=(), aliases=None
):
    return pl.pallas_call(
        kernel,
        out_shape=outs,
        grid_spec=pltpu.PrefetchScalarGridSpec(
            num_scalar_prefetch=1,
            grid=grid,
            in_specs=specs,
            out_specs=[whole(*o.shape) for o in outs] if out_specs is None else out_specs,
            scratch_shapes=scratch,
        ),
        input_output_aliases=aliases or {},
        compiler_params=pltpu.CompilerParams(vmem_limit_bytes=mib * 1024 * 1024),
        cost_estimate=pl.CostEstimate(flops=flops, bytes_accessed=moved, transcendentals=0),
        name=name,
    )


def part(rows, columns, at):
    return pl.BlockSpec((rows, columns), lambda *_: (at, 0))


def shape(rows, columns, dtype):
    return jax.ShapeDtypeStruct((rows, columns), dtype)


def take(place, grads, pieces, owned):
    def kernel(place_ref, g_ref, *refs):
        outs, sems = refs[:-1], refs[-1]
        copies = []
        for k, ((entry, stride, first, rows), out) in enumerate(zip(pieces, outs)):
            for side in range(2):
                block = (place_ref[entry] + side * stride) * owned
                copies.append(
                    pltpu.make_async_copy(
                        g_ref.at[pl.ds(first, rows), pl.ds(pl.multiple_of(block, owned), owned)],
                        out.at[:, pl.ds(side * owned, owned)],
                        sems.at[2 * k + side],
                    )
                )
        for copy in copies:
            copy.start()
        for copy in copies:
            copy.wait()

    outs = [shape(rows, 2 * owned, grads.dtype) for _, _, _, rows in pieces]
    return call(
        kernel,
        "take",
        outs,
        [pl.BlockSpec(memory_space=pl.ANY)],
        8,
        0,
        8 * owned * sum(rows for _, _, _, rows in pieces),
        scratch=[pltpu.SemaphoreType.DMA((2 * len(pieces),))],
    )(place, grads)


def rank_halves(place, activations, basis, core_at, pieces=(1, 3, 4)):
    tokens, depth = activations.shape
    ranks = basis.shape[1] // 2
    unit = depth // sum(pieces)
    ends = [unit * sum(pieces[: k + 1]) for k in range(len(pieces))]
    spans = [slice(end - unit * n, end) for end, n in zip(ends, pieces)]

    def kernel(place_ref, a_hbm, b_hbm, other_ref, own_ref, a_ref, b_ref, total_ref, sems):
        core = place_ref[core_at]
        copies = []
        for k, span in enumerate(spans):
            copies.append(
                (
                    pltpu.make_async_copy(a_hbm.at[:, span], a_ref.at[:, span], sems.at[2 * k]),
                    pltpu.make_async_copy(b_hbm.at[span, :], b_ref.at[span, :], sems.at[2 * k + 1]),
                )
            )
        for pair in copies:
            for copy in pair:
                copy.start()
        for k, (span, pair) in enumerate(zip(spans, copies)):
            for copy in pair:
                copy.wait()
            for o_ref, half in ((total_ref, 1 - core), (own_ref, core)):
                columns = pl.ds(pl.multiple_of(half * ranks, ranks), ranks)
                part = jnp.dot(
                    a_ref[:, span], b_ref[span, columns], preferred_element_type=jnp.float32
                )
                if k:
                    part = o_ref[...] + part
                if k == len(spans) - 1 and o_ref is total_ref:
                    other_ref[...] = part.astype(other_ref.dtype)
                else:
                    o_ref[...] = part

    return call(
        kernel,
        "rank_halves",
        [shape(tokens, ranks, jnp.bfloat16), shape(tokens, ranks, jnp.float32)],
        [pl.BlockSpec(memory_space=pl.ANY)] * 2,
        24,
        4 * tokens * depth * ranks,
        2 * (tokens + 2 * ranks) * depth + 8 * tokens * ranks,
        scratch=[
            pltpu.VMEM((tokens, depth), activations.dtype),
            pltpu.VMEM((depth, 2 * ranks), basis.dtype),
            pltpu.VMEM((tokens, ranks), jnp.float32),
            pltpu.SemaphoreType.DMA((2 * len(pieces),)),
        ],
    )(place, activations, basis)


def added(place, keep, at, parts, terms, masked, mask_at):
    rows, ranks = keep.shape[0] // parts, keep.shape[1]
    operands = [*terms, *masked]
    pieces = max([len(term) for term in operands])
    height = rows // pieces
    flat = [piece for term in operands for piece in term]

    def kernel(place_ref, keep_ref, *refs):
        for k in range(pieces):
            here = slice(k * height, (k + 1) * height)
            total, first = keep_ref[here, :], 0
            for number, term in enumerate(operands):
                own = refs[first : first + len(term)]
                first += len(term)
                value = own[k][...] if len(term) == pieces else own[0][here, :]
                value = value.astype(jnp.float32)
                if number >= len(terms):
                    value = jnp.where(place_ref[mask_at] == 1, value, 0.0)
                total = total + value
            refs[-1][here, :] = total.astype(jnp.bfloat16)

    return call(
        kernel,
        "added",
        [shape(rows, ranks, jnp.bfloat16)],
        [part(rows, ranks, at)] + [whole(*piece.shape) for piece in flat],
        12,
        rows * ranks * len(operands),
        4 * rows * ranks * len(operands),
    )(place, keep, *flat)[0]


def rounded(place, own, arrived):
    def kernel(place_ref, a_ref, b_ref, o_ref):
        o_ref[...] = (a_ref[...] + b_ref[...].astype(jnp.float32)).astype(jnp.bfloat16)

    rows, columns = own.shape
    return call(
        kernel,
        "rounded",
        [shape(rows, columns, jnp.bfloat16)],
        [whole(rows, columns)] * 2,
        12,
        rows * columns,
        10 * rows * columns,
    )(place, own, arrived)[0]


def partial_sums(place, grads, got, rank_own, rank_got, theirs_at, ours_at, side_at, parts):
    tokens, ranks = rank_own[0].shape
    wide = got[0].shape[1]
    owned = wide // 2
    pieces = len(got)
    rows = owned // parts

    def kernel(place_ref, theirs_ref, ours_ref, *refs):
        got_refs, (t0_ref, t1_ref, u0_ref, u1_ref, *send_refs, keep_ref) = refs[:pieces], refs[pieces:]
        mine = jnp.concatenate([theirs_ref[...], ours_ref[...]], axis=1)
        near = place_ref[side_at]
        theirs = pl.ds(pl.multiple_of((1 - near) * owned, owned), owned)
        ours = pl.ds(pl.multiple_of(near * owned, owned), owned)
        far = jnp.concatenate(
            [jnp.concatenate([r[:, theirs], r[:, ours]], axis=1) for r in got_refs], axis=0
        )
        dims = (((0,), (0,)), ((), ()))
        for side, (t_ref, u_ref) in enumerate(((t0_ref, u0_ref), (t1_ref, u1_ref))):
            total = lax.dot_general(
                mine, t_ref[...], dims, preferred_element_type=jnp.float32
            ) + lax.dot_general(far, u_ref[...], dims, preferred_element_type=jnp.float32)
            columns = slice(side * ranks, (side + 1) * ranks)
            for at, send_ref in enumerate(send_refs):
                send_ref[:, columns] = total[at * rows : (at + 1) * rows].astype(send_ref.dtype)
            keep_ref[:, columns] = total[owned:]

    return call(
        kernel,
        "partial_sums",
        [shape(rows, 2 * ranks, jnp.bfloat16)] * parts + [shape(owned, 2 * ranks, jnp.float32)],
        [
            pl.BlockSpec((tokens, owned), lambda i, p: (0, p[theirs_at])),
            pl.BlockSpec((tokens, owned), lambda i, p: (0, p[ours_at])),
        ]
        + [whole(*g.shape) for g in got]
        + [whole(tokens, ranks)] * 4,
        20,
        8 * tokens * wide * ranks,
        4 * tokens * (wide + 2 * ranks) + 12 * owned * ranks,
    )(place, grads, grads, *got, *rank_own, *rank_got)


def moments(place, terms, masked, moment1, moment2, mask_at, core_at, steps=2):
    owned, ranks = moment1.shape
    rows = owned // steps
    count = len(terms)

    def kernel(place_ref, *refs):
        total = refs[0][...].astype(jnp.float32)
        for ref in refs[1:count]:
            total += ref[...].astype(jnp.float32)
        total += jnp.where(place_ref[mask_at] == 1, refs[count][...].astype(jnp.float32), 0.0)
        here, there = total[:, : ranks // 2], total[:, ranks // 2 :]
        first = place_ref[core_at] == 0
        reduced = jnp.concatenate(
            [jnp.where(first, here, there), jnp.where(first, there, here)], axis=1
        )
        m1_ref, m2_ref, first_ref, second_ref, normed_ref = refs[count + 1 :]
        first_ref[...], second_ref[...], normed_ref[...] = adam(reduced, m1_ref[...], m2_ref[...])

    block = pl.BlockSpec((rows, ranks), lambda i, p: (i, 0))
    wide = shape(owned, ranks, jnp.float32)
    return call(
        kernel,
        "moments",
        [wide, wide, shape(owned, ranks, jnp.bfloat16)],
        [block] * (count + 3),
        12,
        20 * owned * ranks,
        28 * owned * ranks,
        out_specs=[block] * 3,
        grid=(steps,),
    )(place, *terms, masked, moment1, moment2)


def update_rows(place, normed, normed_other, basis, core_at, steps=4):
    owned, ranks = normed.shape
    width = basis.shape[0]
    tile = width // steps

    def kernel(place_ref, n_ref, m_ref, b_ref, o_ref):
        core = place_ref[core_at]
        rows = jnp.concatenate([n_ref[...], m_ref[...]])
        here = pl.ds(pl.multiple_of(pl.program_id(0) * tile, tile), tile)
        full = lax.dot_general(
            rows, b_ref[here, :], (((1,), (1,)), ((), ())), preferred_element_type=jnp.float32
        ).astype(jnp.bfloat16)
        o_ref[core] = full[:owned]
        o_ref[1 - core] = full[owned:]

    return call(
        kernel,
        "update_rows",
        [jax.ShapeDtypeStruct((2, owned, width), jnp.bfloat16)],
        [whole(owned, ranks), whole(owned, ranks), pl.BlockSpec(memory_space=pltpu.VMEM)],
        16,
        4 * owned * ranks * width,
        2 * (2 * owned * ranks + width * ranks + 2 * owned * width),
        out_specs=[pl.BlockSpec((2, owned, tile), lambda n, p: (0, 0, n))],
        grid=(steps,),
    )(place, normed, normed_other, basis)[0]


def staged(activations, out_grads, basis, moment1, moment2):
    shards = lax.axis_size("dp")
    planes = shards // 4
    owned = moment1.shape[0]
    tokens = activations.shape[0]
    me, core = lax.axis_index("dp"), lax.axis_index("mp")
    z, y, x = me // 4, me // 2 % 2, me % 2
    mid = (z > 0) & (z < planes - 1)

    along_y = [(i, i ^ 2) for i in range(shards)]
    along_x = [(i, i ^ 1) for i in range(shards)]
    outer = [(i, i ^ 4) for i in range(shards)]
    inner = [
        (2 * i + k, 2 * (i ^ 12) + k if 4 <= i < shards - 4 else 2 * i + 1 - k)
        for i in range(shards)
        for k in range(2)
    ]
    cores = [(0, 1), (1, 0)]

    order = [
        sorted(
            range(planes),
            key=lambda d, p=p: (d == p, -abs(d - p), (d < p) == (p < planes // 2)),
        )
        for p in range(planes)
    ]
    blocks = [
        sum(jnp.where(z == p, order[p][c], 0) for p in range(planes)) for c in range(planes)
    ]
    first_y = [c != 1 for c in range(planes)]
    base = [b * 4 + ((1 - y) * 2 if f else 1 - x) for b, f in zip(blocks, first_y)]
    ours = [b * 4 + y * 2 + x for b in blocks]
    theirs = [b * 4 + (y * 2 + 1 - x if f else (1 - y) * 2 + x) for b, f in zip(blocks, first_y)]
    place = jnp.stack([*base, *ours, *theirs, x, y, core, mid]).astype(jnp.int32)
    ours_at, theirs_at = planes, 2 * planes
    x_at, y_at, core_at, mid_at = range(3 * planes, 3 * planes + 4)

    def piece(c, first=0, rows=tokens):
        return c, 1 if first_y[c] else 2, first, rows

    def raw(c, mine):
        return lax.ppermute(mine, "dp", along_y if first_y[c] else along_x)

    grads, basis_hbm = (pltpu.with_memory_space_constraint(a, pltpu.HBM) for a in (out_grads, basis))
    early = take(place, grads, [piece(0), piece(1)], owned)
    activations, *early = lax.optimization_barrier((activations, *early))
    first, second = (raw(c, mine) for c, mine in enumerate(early))

    activations = pltpu.with_memory_space_constraint(activations, pltpu.HBM)
    other, own = rank_halves(place, activations, basis_hbm, core_at)
    other, own, first = lax.optimization_barrier((other, own, first))
    arrived = lax.ppermute(other, "mp", cores)
    arrived, second = lax.optimization_barrier((arrived, second))
    half = rounded(place, own, arrived)
    half_y = lax.ppermute(half, "dp", along_y)
    half_x = lax.ppermute(half, "dp", along_x)
    half_other = lax.ppermute(half, "mp", cores)
    place_later, _ = lax.optimization_barrier((place, half))
    rest = take(place_later, grads, [piece(c) for c in range(2, planes)], owned)
    half_y, *rest = lax.optimization_barrier((half_y, *rest))
    got = [[first], [second]] + [
        [raw(c, mine)] for c, mine in enumerate(rest, 2)
    ]
    rank_own = (half, half_other)
    rank_y = (half_y, lax.ppermute(half_y, "mp", cores))
    rank_x = (half_x, lax.ppermute(half_x, "mp", cores))

    parts = [2, 1, 1, 1]
    keeps, arrivals, now = {}, {}, [place]

    def then(result):
        return result

    def block(c):
        *sends, keeps[c] = then(
            partial_sums(
                now[0],
                grads,
                got[c],
                rank_own,
                rank_y if first_y[c] else rank_x,
                theirs_at + c,
                ours_at + c,
                x_at if first_y[c] else y_at,
                parts[c],
            )
        )
        second = along_x if first_y[c] else along_y
        arrivals[c] = [lax.ppermute(send, "dp", second) for send in sends]

    def hop(c, at, of, axes, pairs, terms=(), masked=()):
        come = arrivals[c] if of == 1 else [arrivals[c][at]]
        value = then(added(now[0], keeps[c], at, of, [come, *terms], masked, mid_at))
        return lax.ppermute(value, axes, pairs)

    both = ("dp", "mp")
    block(0)
    block(1)
    out1 = [hop(0, at, parts[0], "dp", outer) for at in range(parts[0])]
    block(2)
    in2 = hop(0, 0, 1, both, inner, [out1])
    out2 = hop(1, 0, 1, "dp", outer)
    block(3)
    out3 = hop(2, 0, 1, "dp", outer, masked=[[in2]])
    in3 = hop(1, 0, 1, both, inner, [[out2]])
    new_first, new_second, normed = moments(
        now[0], [keeps[3], *arrivals[3], out3], in3, moment1, moment2, mid_at, core_at
    )
    normed_other = lax.ppermute(normed, "mp", cores)
    update = update_rows(place, normed, normed_other, basis, core_at)
    return new_first, new_second, update


def solution(mesh):
    fits = mesh.shape["mp"] == 2 and mesh.shape["dp"] == 16
    return jax.shard_map(
        staged if fits else plain,
        mesh=mesh,
        in_specs=(
            P("dp", "mp"),
            P("dp", "mp"),
            P("mp", None),
            P(("mp", "dp"), None),
            P(("mp", "dp"), None),
        ),
        out_specs=(P(("mp", "dp"), None), P(("mp", "dp"), None), P(None, "dp", "mp")),
        check_vma=False,
    )
```

```python
import jax
import jax.numpy as jnp
from jax import lax
from jax.experimental import pallas as pl
from jax.experimental.pallas import tpu as pltpu
from jax.sharding import PartitionSpec as P

STEP = 100


beta_first = 0.9
beta_second = 0.999
epsilon = 1e-08


def adam(reduced, moment1, moment2):
    new_first = beta_first * moment1 + (1.0 - beta_first) * reduced
    new_second = beta_second * moment2 + (1.0 - beta_second) * reduced * reduced
    bias_first = 1.0 - beta_first**STEP
    bias_second = 1.0 - beta_second**STEP
    normed = (new_first / bias_first / (jnp.sqrt(new_second / bias_second) + epsilon)).astype(
        jnp.bfloat16
    )
    return new_first, new_second, normed


def plain(activations, out_grads, basis, moment1, moment2):
    partial_rank = jnp.dot(activations, basis, preferred_element_type=jnp.float32)
    token_rank = lax.psum(partial_rank, "mp").astype(jnp.bfloat16)
    reduced = lax.psum_scatter(
        lax.dot_general(
            out_grads, token_rank, (((0,), (0,)), ((), ())), preferred_element_type=jnp.float32
        ),
        "dp",
        scatter_dimension=0,
        tiled=True,
    )
    new_first, new_second, normed = adam(reduced, moment1, moment2)
    gathered = lax.all_gather(normed[None], "mp", axis=0, tiled=True)
    groups, owned, ranks = gathered.shape
    full = lax.dot_general(
        gathered.reshape(groups * owned, ranks),
        basis,
        (((1,), (1,)), ((), ())),
        preferred_element_type=jnp.float32,
    )
    return new_first, new_second, full.astype(jnp.bfloat16).reshape(groups, owned, basis.shape[0])


def whole(rows, columns):
    return pl.BlockSpec((rows, columns), lambda *_: (0, 0))


def call(
    kernel, name, outs, specs, mib, flops, moved, out_specs=None, grid=(1,), scratch=(), aliases=None
):
    return pl.pallas_call(
        kernel,
        out_shape=outs,
        grid_spec=pltpu.PrefetchScalarGridSpec(
            num_scalar_prefetch=1,
            grid=grid,
            in_specs=specs,
            out_specs=[whole(*o.shape) for o in outs] if out_specs is None else out_specs,
            scratch_shapes=scratch,
        ),
        input_output_aliases=aliases or {},
        compiler_params=pltpu.CompilerParams(vmem_limit_bytes=mib * 1024 * 1024),
        cost_estimate=pl.CostEstimate(flops=flops, bytes_accessed=moved, transcendentals=0),
        name=name,
    )


def part(rows, columns, at):
    return pl.BlockSpec((rows, columns), lambda *_: (at, 0))


def shape(rows, columns, dtype):
    return jax.ShapeDtypeStruct((rows, columns), dtype)


def take(place, grads, pieces, owned):
    def kernel(place_ref, g_ref, *refs):
        outs, sems = refs[:-1], refs[-1]
        copies = []
        for k, ((entry, stride, first, rows), out) in enumerate(zip(pieces, outs)):
            for side in range(2):
                block = (place_ref[entry] + side * stride) * owned
                copies.append(
                    pltpu.make_async_copy(
                        g_ref.at[pl.ds(first, rows), pl.ds(pl.multiple_of(block, owned), owned)],
                        out.at[:, pl.ds(side * owned, owned)],
                        sems.at[2 * k + side],
                    )
                )
        for copy in copies:
            copy.start()
        for copy in copies:
            copy.wait()

    outs = [shape(rows, 2 * owned, grads.dtype) for _, _, _, rows in pieces]
    return call(
        kernel,
        "take",
        outs,
        [pl.BlockSpec(memory_space=pl.ANY)],
        8,
        0,
        8 * owned * sum(rows for _, _, _, rows in pieces),
        scratch=[pltpu.SemaphoreType.DMA((2 * len(pieces),))],
    )(place, grads)


def rank_halves(place, activations, basis, core_at, pieces=(1, 3, 4)):
    tokens, depth = activations.shape
    ranks = basis.shape[1] // 2
    unit = depth // sum(pieces)
    ends = [unit * sum(pieces[: k + 1]) for k in range(len(pieces))]
    spans = [slice(end - unit * n, end) for end, n in zip(ends, pieces)]

    def kernel(place_ref, a_hbm, b_hbm, other_ref, own_ref, a_ref, b_ref, total_ref, sems):
        core = place_ref[core_at]
        copies = []
        for k, span in enumerate(spans):
            copies.append(
                (
                    pltpu.make_async_copy(a_hbm.at[:, span], a_ref.at[:, span], sems.at[2 * k]),
                    pltpu.make_async_copy(b_hbm.at[span, :], b_ref.at[span, :], sems.at[2 * k + 1]),
                )
            )
        for pair in copies:
            for copy in pair:
                copy.start()
        for k, (span, pair) in enumerate(zip(spans, copies)):
            for copy in pair:
                copy.wait()
            for o_ref, half in ((total_ref, 1 - core), (own_ref, core)):
                columns = pl.ds(pl.multiple_of(half * ranks, ranks), ranks)
                part = jnp.dot(
                    a_ref[:, span], b_ref[span, columns], preferred_element_type=jnp.float32
                )
                if k:
                    part = o_ref[...] + part
                if k == len(spans) - 1 and o_ref is total_ref:
                    other_ref[...] = part.astype(other_ref.dtype)
                else:
                    o_ref[...] = part

    return call(
        kernel,
        "rank_halves",
        [shape(tokens, ranks, jnp.bfloat16), shape(tokens, ranks, jnp.float32)],
        [pl.BlockSpec(memory_space=pl.ANY)] * 2,
        24,
        4 * tokens * depth * ranks,
        2 * (tokens + 2 * ranks) * depth + 8 * tokens * ranks,
        scratch=[
            pltpu.VMEM((tokens, depth), activations.dtype),
            pltpu.VMEM((depth, 2 * ranks), basis.dtype),
            pltpu.VMEM((tokens, ranks), jnp.float32),
            pltpu.SemaphoreType.DMA((2 * len(pieces),)),
        ],
    )(place, activations, basis)


def added(place, keep, at, parts, terms, masked, mask_at):
    rows, ranks = keep.shape[0] // parts, keep.shape[1]
    operands = [*terms, *masked]
    pieces = max([len(term) for term in operands])
    height = rows // pieces
    flat = [piece for term in operands for piece in term]

    def kernel(place_ref, keep_ref, *refs):
        for k in range(pieces):
            here = slice(k * height, (k + 1) * height)
            total, first = keep_ref[here, :], 0
            for number, term in enumerate(operands):
                own = refs[first : first + len(term)]
                first += len(term)
                value = own[k][...] if len(term) == pieces else own[0][here, :]
                value = value.astype(jnp.float32)
                if number >= len(terms):
                    value = jnp.where(place_ref[mask_at] == 1, value, 0.0)
                total = total + value
            refs[-1][here, :] = total.astype(jnp.bfloat16)

    return call(
        kernel,
        "added",
        [shape(rows, ranks, jnp.bfloat16)],
        [part(rows, ranks, at)] + [whole(*piece.shape) for piece in flat],
        12,
        rows * ranks * len(operands),
        4 * rows * ranks * len(operands),
    )(place, keep, *flat)[0]


def rounded(place, own, arrived):
    def kernel(place_ref, a_ref, b_ref, o_ref):
        o_ref[...] = (a_ref[...] + b_ref[...].astype(jnp.float32)).astype(jnp.bfloat16)

    rows, columns = own.shape
    return call(
        kernel,
        "rounded",
        [shape(rows, columns, jnp.bfloat16)],
        [whole(rows, columns)] * 2,
        12,
        rows * columns,
        10 * rows * columns,
    )(place, own, arrived)[0]


def partial_sums(place, grads, got, rank_own, rank_got, theirs_at, ours_at, side_at, parts):
    tokens, ranks = rank_own[0].shape
    wide = got[0].shape[1]
    owned = wide // 2
    pieces = len(got)
    rows = owned // parts

    def kernel(place_ref, theirs_ref, ours_ref, *refs):
        got_refs, (t0_ref, t1_ref, u0_ref, u1_ref, *send_refs, keep_ref) = refs[:pieces], refs[pieces:]
        mine = jnp.concatenate([theirs_ref[...], ours_ref[...]], axis=1)
        near = place_ref[side_at]
        theirs = pl.ds(pl.multiple_of((1 - near) * owned, owned), owned)
        ours = pl.ds(pl.multiple_of(near * owned, owned), owned)
        far = jnp.concatenate(
            [jnp.concatenate([r[:, theirs], r[:, ours]], axis=1) for r in got_refs], axis=0
        )
        dims = (((0,), (0,)), ((), ()))
        for side, (t_ref, u_ref) in enumerate(((t0_ref, u0_ref), (t1_ref, u1_ref))):
            total = lax.dot_general(
                mine, t_ref[...], dims, preferred_element_type=jnp.float32
            ) + lax.dot_general(far, u_ref[...], dims, preferred_element_type=jnp.float32)
            columns = slice(side * ranks, (side + 1) * ranks)
            for at, send_ref in enumerate(send_refs):
                send_ref[:, columns] = total[at * rows : (at + 1) * rows].astype(send_ref.dtype)
            keep_ref[:, columns] = total[owned:]

    return call(
        kernel,
        "partial_sums",
        [shape(rows, 2 * ranks, jnp.bfloat16)] * parts + [shape(owned, 2 * ranks, jnp.float32)],
        [
            pl.BlockSpec((tokens, owned), lambda i, p: (0, p[theirs_at])),
            pl.BlockSpec((tokens, owned), lambda i, p: (0, p[ours_at])),
        ]
        + [whole(*g.shape) for g in got]
        + [whole(tokens, ranks)] * 4,
        20,
        8 * tokens * wide * ranks,
        4 * tokens * (wide + 2 * ranks) + 12 * owned * ranks,
    )(place, grads, grads, *got, *rank_own, *rank_got)


def moments(place, terms, masked, moment1, moment2, mask_at, core_at, steps=2):
    owned, ranks = moment1.shape
    rows = owned // steps
    count = len(terms)

    def kernel(place_ref, *refs):
        total = refs[0][...].astype(jnp.float32)
        for ref in refs[1:count]:
            total += ref[...].astype(jnp.float32)
        total += jnp.where(place_ref[mask_at] == 1, refs[count][...].astype(jnp.float32), 0.0)
        here, there = total[:, : ranks // 2], total[:, ranks // 2 :]
        first = place_ref[core_at] == 0
        reduced = jnp.concatenate(
            [jnp.where(first, here, there), jnp.where(first, there, here)], axis=1
        )
        m1_ref, m2_ref, first_ref, second_ref, normed_ref = refs[count + 1 :]
        first_ref[...], second_ref[...], normed_ref[...] = adam(reduced, m1_ref[...], m2_ref[...])

    block = pl.BlockSpec((rows, ranks), lambda i, p: (i, 0))
    wide = shape(owned, ranks, jnp.float32)
    return call(
        kernel,
        "moments",
        [wide, wide, shape(owned, ranks, jnp.bfloat16)],
        [block] * (count + 3),
        12,
        20 * owned * ranks,
        28 * owned * ranks,
        out_specs=[block] * 3,
        grid=(steps,),
    )(place, *terms, masked, moment1, moment2)


def update_rows(place, normed, normed_other, basis, core_at, steps=4):
    owned, ranks = normed.shape
    width = basis.shape[0]
    tile = width // steps

    def kernel(place_ref, n_ref, m_ref, b_ref, o_ref):
        core = place_ref[core_at]
        rows = jnp.concatenate([n_ref[...], m_ref[...]])
        here = pl.ds(pl.multiple_of(pl.program_id(0) * tile, tile), tile)
        full = lax.dot_general(
            rows, b_ref[here, :], (((1,), (1,)), ((), ())), preferred_element_type=jnp.float32
        ).astype(jnp.bfloat16)
        o_ref[core] = full[:owned]
        o_ref[1 - core] = full[owned:]

    return call(
        kernel,
        "update_rows",
        [jax.ShapeDtypeStruct((2, owned, width), jnp.bfloat16)],
        [whole(owned, ranks), whole(owned, ranks), pl.BlockSpec(memory_space=pltpu.VMEM)],
        16,
        4 * owned * ranks * width,
        2 * (2 * owned * ranks + width * ranks + 2 * owned * width),
        out_specs=[pl.BlockSpec((2, owned, tile), lambda n, p: (0, 0, n))],
        grid=(steps,),
    )(place, normed, normed_other, basis)[0]


def staged(activations, out_grads, basis, moment1, moment2):
    shards = lax.axis_size("dp")
    planes = shards // 4
    owned = moment1.shape[0]
    tokens = activations.shape[0]
    me, core = lax.axis_index("dp"), lax.axis_index("mp")
    z, y, x = me // 4, me // 2 % 2, me % 2
    mid = (z > 0) & (z < planes - 1)

    along_y = [(i, i ^ 2) for i in range(shards)]
    along_x = [(i, i ^ 1) for i in range(shards)]
    outer = [(i, i ^ 4) for i in range(shards)]
    inner = [
        (2 * i + k, 2 * (i ^ 12) + k if 4 <= i < shards - 4 else 2 * i + 1 - k)
        for i in range(shards)
        for k in range(2)
    ]
    cores = [(0, 1), (1, 0)]

    order = [
        sorted(
            range(planes),
            key=lambda d, p=p: (d == p, -abs(d - p), (d < p) == (p < planes // 2)),
        )
        for p in range(planes)
    ]
    blocks = [
        sum(jnp.where(z == p, order[p][c], 0) for p in range(planes)) for c in range(planes)
    ]
    first_y = [c != 1 for c in range(planes)]
    base = [b * 4 + ((1 - y) * 2 if f else 1 - x) for b, f in zip(blocks, first_y)]
    ours = [b * 4 + y * 2 + x for b in blocks]
    theirs = [b * 4 + (y * 2 + 1 - x if f else (1 - y) * 2 + x) for b, f in zip(blocks, first_y)]
    place = jnp.stack([*base, *ours, *theirs, x, y, core, mid]).astype(jnp.int32)
    ours_at, theirs_at = planes, 2 * planes
    x_at, y_at, core_at, mid_at = range(3 * planes, 3 * planes + 4)

    def piece(c, first=0, rows=tokens):
        return c, 1 if first_y[c] else 2, first, rows

    def raw(c, mine):
        return lax.ppermute(mine, "dp", along_y if first_y[c] else along_x)

    grads, basis_hbm = (pltpu.with_memory_space_constraint(a, pltpu.HBM) for a in (out_grads, basis))
    early = take(place, grads, [piece(0), piece(1)], owned)
    activations, *early = lax.optimization_barrier((activations, *early))
    first, second = (raw(c, mine) for c, mine in enumerate(early))

    activations = pltpu.with_memory_space_constraint(activations, pltpu.HBM)
    other, own = rank_halves(place, activations, basis_hbm, core_at)
    other, own, first = lax.optimization_barrier((other, own, first))
    arrived = lax.ppermute(other, "mp", cores)
    arrived, second = lax.optimization_barrier((arrived, second))
    half = rounded(place, own, arrived)
    half_y = lax.ppermute(half, "dp", along_y)
    half_x = lax.ppermute(half, "dp", along_x)
    half_other = lax.ppermute(half, "mp", cores)
    place_later, _ = lax.optimization_barrier((place, half))
    rest = take(place_later, grads, [piece(c) for c in range(2, planes)], owned)
    half_y, *rest = lax.optimization_barrier((half_y, *rest))
    got = [[first], [second]] + [
        [raw(c, mine)] for c, mine in enumerate(rest, 2)
    ]
    rank_own = (half, half_other)
    rank_y = (half_y, lax.ppermute(half_y, "mp", cores))
    rank_x = (half_x, lax.ppermute(half_x, "mp", cores))

    parts = [2, 1, 1, 1]
    keeps, arrivals, now = {}, {}, [place]

    def then(result):
        now[0], _ = lax.optimization_barrier((now[0], result))
        return result

    def block(c):
        *sends, keeps[c] = then(
            partial_sums(
                now[0],
                grads,
                got[c],
                rank_own,
                rank_y if first_y[c] else rank_x,
                theirs_at + c,
                ours_at + c,
                x_at if first_y[c] else y_at,
                parts[c],
            )
        )
        second = along_x if first_y[c] else along_y
        arrivals[c] = [lax.ppermute(send, "dp", second) for send in sends]

    def hop(c, at, of, axes, pairs, terms=(), masked=()):
        come = arrivals[c] if of == 1 else [arrivals[c][at]]
        value = then(added(now[0], keeps[c], at, of, [come, *terms], masked, mid_at))
        return lax.ppermute(value, axes, pairs)

    both = ("dp", "mp")
    block(0)
    block(1)
    out1 = [hop(0, 0, parts[0], "dp", outer)]
    out1.append(hop(0, 1, parts[0], "dp", outer))
    block(2)
    in2 = [hop(0, 0, parts[0], both, inner, [[out1[0]]])]
    in2.append(hop(0, 1, parts[0], both, inner, [[out1[1]]]))
    out2 = hop(1, 0, 1, "dp", outer)
    block(3)
    out3 = hop(2, 0, 1, "dp", outer, masked=[in2])
    in3 = hop(1, 0, 1, both, inner, [[out2]])
    new_first, new_second, normed = moments(
        now[0], [keeps[3], *arrivals[3], out3], in3, moment1, moment2, mid_at, core_at
    )
    normed_other = lax.ppermute(normed, "mp", cores)
    update = update_rows(place, normed, normed_other, basis, core_at)
    return new_first, new_second, update


def solution(mesh):
    fits = mesh.shape["mp"] == 2 and mesh.shape["dp"] == 16
    return jax.shard_map(
        staged if fits else plain,
        mesh=mesh,
        in_specs=(
            P("dp", "mp"),
            P("dp", "mp"),
            P("mp", None),
            P(("mp", "dp"), None),
            P(("mp", "dp"), None),
        ),
        out_specs=(P(("mp", "dp"), None), P(("mp", "dp"), None), P(None, "dp", "mp")),
        check_vma=False,
    )
```
